32 devices in a mesh: ctx: 16 (over z, y, core), head: 2 (over x).
Axes of the slice: x: 2, y: 2, z: 4, core: 2. Of those that a mesh axis runs over, the one named last changes fastest.
Arguments:
- queries: bfloat16 [2048, 2048], P('ctx', 'head'), may hold values from -6 to 6
- key_states: bfloat16 [2048, 512], P(('ctx', 'head')), may hold values from -6 to 6
- value_states: bfloat16 [2048, 512], P(('ctx', 'head')), may hold values from -6 to 6
- attn_out: bfloat16 [2048, 2048], P('ctx', 'head'), may hold values from -1.5 to 1.5
- grad_out: bfloat16 [2048, 2048], P('ctx', 'head'), may hold values from -24 to 24
- log_sum_exp: float32 [16, 2048], P('head', 'ctx')
- token_order: int32 [2048], P('ctx'), may hold values from 0 to 2047, as said below
- position: int32 [2048], P('ctx'), may hold values from 0 to 511, as said below
Outputs:
- grad_queries: bfloat16 [2048, 2048], P('ctx', 'head')
- grad_keys: bfloat16 [2048, 512], P(('ctx', 'head'))
- grad_values: bfloat16 [2048, 512], P(('ctx', 'head'))
The draws below stay inside these ranges and needn't reach their ends.
Inputs may be any that keep to these rules, and one draw needn't show every extreme that they name: `token_order`: a permutation of the sequence positions; the 128 rows of ctx index d hold consecutive positions in increasing order, all within quarter d mod 4 of the sequence (quarter k holds positions k * 512 to (k + 1) * 512 - 1). Documents are runs of consecutive sequence positions that never cross a multiple of 512; token_order[r] - position[r] is the sequence position where row r's document starts; some document fills a whole quarter.
All inputs are finite; a program needn't handle non-finite values.
Results may differ from the reference program's by a relative error of at most 0.0055.
Values may be sent and summed in bfloat16 or wider, within the bound.
A program may use at most 64 MiB of HBM per device.

```python
import math
import jax
import jax.numpy as jnp
from jax import lax

HEAD_DIM = 128
HEADS = 16
KV_HEADS = 4
TOK_DEV = 128
TOKENS = 2048


def layout_tables(base_key):
    block_count = TOKENS // TOK_DEV
    per_quarter = block_count // 4
    raw = jax.random.randint(jax.random.fold_in(base_key, 101), (4, per_quarter), 0, 1 << 20, dtype=jnp.int32)
    distinct = raw * per_quarter + jnp.arange(per_quarter, dtype=jnp.int32)[None, :]
    ranks = jnp.argsort(distinct, axis=1, stable=True).astype(jnp.int32)
    quarter_base = jnp.arange(4, dtype=jnp.int32)[None, :] * per_quarter
    chosen = (quarter_base + jnp.transpose(ranks)).reshape(block_count)
    within = jnp.arange(TOK_DEV, dtype=jnp.int32)
    order_table = (chosen[:, None] * TOK_DEV + within[None, :]).reshape(TOKENS)
    random_cuts = jax.random.randint(jax.random.fold_in(base_key, 102), (3,), 1, TOKENS, dtype=jnp.int32)
    quarter_cuts = jnp.array([1, 2, 3], dtype=jnp.int32) * (TOKENS // 4)
    cuts = jnp.concatenate([random_cuts, quarter_cuts])
    places = jnp.arange(TOKENS, dtype=jnp.int32)
    starts = jnp.max(jnp.where(cuts[None, :] <= places[:, None], cuts[None, :], 0), axis=1)
    offsets = places - starts
    return (order_table, offsets[order_table])


def draw_token_order(key, part):
    return layout_tables(key)[0]


def draw_position(key, part):
    return layout_tables(key)[1]


def draw_log_sum_exp(key, part):
    offsets = layout_tables(key)[1]
    centre = jnp.log(offsets.astype(jnp.float32) + 1.0) + 0.5
    noise_key = jax.random.fold_in(key, 103)
    noise = jax.random.uniform(noise_key, (HEADS, TOKENS), jnp.float32, -0.5, 0.5)
    return (centre[None, :] + noise).astype(jnp.float32)


def levels(rng, shape, cuts, least, largest):
    gain = 1.0
    for axis_at, parts in cuts:
        draws = jax.random.uniform(jax.random.fold_in(jax.random.fold_in(rng, 6), axis_at), (parts,), jnp.float32, least / len(cuts), largest / len(cuts))
        gain = gain * jnp.repeat(jnp.exp(draws), shape[axis_at] // parts).reshape((-1,) + (1,) * (len(shape) - 1 - axis_at))
    return gain


def normal_values(rng, extent, scale, bound, split=(), held_as=jnp.bfloat16):
    factor_of = levels(rng, extent, split, -0.22, 0.18) if split else 1.0
    values = jax.random.normal(rng, extent, jnp.float32) * scale * factor_of
    return jnp.minimum(jnp.maximum(values, -bound), bound).astype(held_as)


def setup_inputs(seed: int = 0) -> dict:
    keys = jax.random.split(jax.random.key(seed), 9)
    queries = normal_values(keys[0], (TOKENS, HEADS * HEAD_DIM), 1.0, 6.0, ((0, 16), (1, 2)))
    key_states = normal_values(keys[1], (TOKENS, KV_HEADS * HEAD_DIM), 1.0, 6.0, ((0, 32),))
    value_states = normal_values(keys[2], (TOKENS, KV_HEADS * HEAD_DIM), 1.0, 6.0, ((0, 32),))
    attn_out = normal_values(keys[3], (TOKENS, HEADS * HEAD_DIM), 0.25, 1.5, ((0, 16), (1, 2)))
    grad_out = normal_values(keys[4], (TOKENS, HEADS * HEAD_DIM), 4.0, 24.0, ((0, 16), (1, 2)))
    log_sum_exp = draw_log_sum_exp(jax.random.fold_in(keys[8], 71), 0)
    token_order = draw_token_order(jax.random.fold_in(keys[8], 71), 0)
    position = draw_position(jax.random.fold_in(keys[8], 71), 0)
    return dict(queries=queries, key_states=key_states, value_states=value_states, attn_out=attn_out, grad_out=grad_out, log_sum_exp=log_sum_exp, token_order=token_order, position=position)


def reference(queries, key_states, value_states, attn_out, grad_out, log_sum_exp, token_order, position):
    group_size = HEADS // KV_HEADS
    score_scale = HEAD_DIM ** -0.5
    tokens = queries.shape[0]
    query_four = queries.astype(jnp.float32).reshape(tokens, KV_HEADS, group_size, HEAD_DIM)
    grad_four = grad_out.astype(jnp.float32).reshape(tokens, KV_HEADS, group_size, HEAD_DIM)
    output_four = attn_out.astype(jnp.float32).reshape(tokens, KV_HEADS, group_size, HEAD_DIM)
    out_dot = jnp.sum(grad_four * output_four, axis=3)
    keys_three = key_states.astype(jnp.float32).reshape(tokens, KV_HEADS, HEAD_DIM)
    values_three = value_states.astype(jnp.float32).reshape(tokens, KV_HEADS, HEAD_DIM)
    lse_three = log_sum_exp.reshape(KV_HEADS, group_size, tokens)
    first_seen = token_order - position
    block_rows = math.gcd(tokens, 256)
    highest = lax.Precision.HIGHEST

    def block_step(sums, block_index):
        key_sum, value_sum = sums
        offset = (block_index * block_rows).astype(jnp.int32)
        query_block = lax.dynamic_slice_in_dim(query_four, offset, block_rows)
        grad_block = lax.dynamic_slice_in_dim(grad_four, offset, block_rows)
        dot_block = lax.dynamic_slice_in_dim(out_dot, offset, block_rows)
        lse_block = lax.dynamic_slice_in_dim(lse_three, offset, block_rows, axis=2)
        last_block = lax.dynamic_slice_in_dim(token_order, offset, block_rows)
        first_block = lax.dynamic_slice_in_dim(first_seen, offset, block_rows)
        visible = (token_order[None, :] <= last_block[:, None]) & (token_order[None, :] >= first_block[:, None])
        scores = jnp.einsum("tkgd,nkd->kgtn", query_block, keys_three, precision=highest) * score_scale
        weights = jnp.where(visible[None, None], jnp.exp(scores - lse_block[..., None]), 0.0)
        weights_round = lax.optimization_barrier(weights.astype(jnp.bfloat16)).astype(jnp.float32)
        prob_grad = jnp.einsum("tkgd,nkd->kgtn", grad_block, values_three, precision=highest)
        dot_moved = jnp.transpose(dot_block, (1, 2, 0))
        score_grad = weights * (prob_grad - dot_moved[..., None]) * score_scale
        score_grad = lax.optimization_barrier(score_grad.astype(jnp.bfloat16)).astype(jnp.float32)
        query_grad = jnp.einsum("kgtn,nkd->tkgd", score_grad, keys_three, precision=highest)
        key_sum = key_sum + jnp.einsum("kgtn,tkgd->nkd", score_grad, query_block, precision=highest)
        value_sum = value_sum + jnp.einsum("kgtn,tkgd->nkd", weights_round, grad_block, precision=highest)
        return (key_sum, value_sum), query_grad

    zeros_three = jnp.zeros((tokens, KV_HEADS, HEAD_DIM), jnp.float32)
    indices = jnp.arange(tokens // block_rows, dtype=jnp.int32)
    sums, query_blocks = lax.scan(block_step, (zeros_three, zeros_three), indices)
    grad_queries = query_blocks.reshape(tokens, HEADS * HEAD_DIM).astype(jnp.bfloat16)
    grad_keys = sums[0].reshape(tokens, KV_HEADS * HEAD_DIM).astype(jnp.bfloat16)
    grad_values = sums[1].reshape(tokens, KV_HEADS * HEAD_DIM).astype(jnp.bfloat16)
    return (grad_queries, grad_keys, grad_values)
```

```python
import functools

import jax
import jax.numpy as jnp
from jax import lax
from jax.experimental import pallas as pl
from jax.experimental.pallas import tpu as pltpu
from jax.sharding import PartitionSpec as P

HEAD_DIM = 128
QUARTERS = 4
MESH = pl.DeviceIdType.MESH


def dot(a, b, dims):
    return lax.dot_general(a, b, (dims, ((), ())), preferred_element_type=jnp.float32)


def kernel(
    members, groups,
    q_hbm, k_hbm, v_hbm, o_hbm, g_hbm, lse_ref, order_ref, pos_ref,
    dq_hbm, dk_hbm, dv_hbm,
    q_buf, o_buf, g_buf, q_tall, g_tall, k_all, v_all, order_all,
    lse_wide, dot_wide, ds_all, k_part, v_part, k_in, v_in, dq_buf, dk_buf, dv_buf,
    local_sem, send_kv, recv_kv, send_order, recv_order, send_grad, recv_grad,
):
    ctx, mine = lax.axis_index("ctx"), lax.axis_index("head")
    me, quarter = ctx // QUARTERS, lax.rem(ctx, QUARTERS)
    own = k_hbm.shape[0]
    rows = q_hbm.shape[0]
    kv_columns = k_hbm.shape[1] // groups
    kv_local = kv_columns // HEAD_DIM
    group_size = q_hbm.shape[1] // kv_columns
    wide = group_size * rows
    scale = HEAD_DIM ** (-0.5)

    def loop(low, high, body):
        if members <= 4:
            for step in range(low, high):
                body(step)
        else:
            def call(step, carry):
                body(step)
                return carry
            lax.fori_loop(low, high, call, 0)

    def device(member, head):
        return (member * QUARTERS + quarter, head)

    def member_at(step):
        return lax.rem(me + step, members)

    def head_at(step):
        return lax.rem(mine + step, groups)

    def columns(head):
        return pl.ds(pl.multiple_of(head * kv_columns, kv_columns), kv_columns)

    def half(head):
        return pl.ds(pl.multiple_of(head * own, own), own)

    def kv_copy(which, member, head, sender, sender_head):
        source = (k_hbm, v_hbm)[which]
        target = (k_all, v_all)[which]
        return pltpu.make_async_remote_copy(
            src_ref=source.at[:, columns(head)],
            dst_ref=target.at[sender, half(sender_head)],
            send_sem=send_kv.at[which, member, head],
            recv_sem=recv_kv.at[which, sender, sender_head],
            device_id=device(member, head),
            device_id_type=MESH,
        )

    def order_copy(member, sender):
        return pltpu.make_async_remote_copy(
            src_ref=order_ref,
            dst_ref=order_all.at[sender],
            send_sem=send_order.at[member],
            recv_sem=recv_order.at[sender],
            device_id=device(member, mine),
            device_id_type=MESH,
        )

    def grad_copy(which, member, head, sender, sender_head):
        source = (k_part, v_part)[which]
        target = (k_in, v_in)[which]
        return pltpu.make_async_remote_copy(
            src_ref=source.at[member, half(head)],
            dst_ref=target.at[sender, :, columns(sender_head)],
            send_sem=send_grad.at[which, member, head],
            recv_sem=recv_grad.at[which, sender, sender_head],
            device_id=device(member, head),
            device_id_type=MESH,
        )

    loads = [
        pltpu.make_async_copy(k_hbm.at[:, columns(mine)], k_all.at[me, half(mine)], local_sem.at[0]),
        pltpu.make_async_copy(v_hbm.at[:, columns(mine)], v_all.at[me, half(mine)], local_sem.at[1]),
        pltpu.make_async_copy(q_hbm, q_buf, local_sem.at[2]),
        pltpu.make_async_copy(o_hbm, o_buf, local_sem.at[3]),
        pltpu.make_async_copy(g_hbm, g_buf, local_sem.at[4]),
    ]
    for load in loads:
        load.start()

    barrier = pltpu.get_barrier_semaphore()

    def greet(step):
        for head_step in range(groups):
            def signal():
                pl.semaphore_signal(
                    barrier, inc=1, device_id=device(member_at(step), head_at(head_step)),
                    device_id_type=MESH,
                )
            signal()

    for head_step in range(1, groups):
        pl.semaphore_signal(
            barrier, inc=1, device_id=device(me, head_at(head_step)), device_id_type=MESH
        )
    loop(1, members, greet)
    pl.semaphore_wait(barrier, members * groups - 1)

    def push(step):
        member = member_at(step)
        order_copy(member, me).start()
        for head_step in range(groups):
            for which in range(2):
                kv_copy(which, member, head_at(head_step), me, mine).start()

    loop(1, members, push)
    for head_step in range(1, groups):
        for which in range(2):
            kv_copy(which, me, head_at(head_step), me, mine).start()

    for load in loads:
        load.wait()
    for head in range(group_size * kv_local):
        kv_head, place = head // group_size, head % group_size
        spot = slice(place * rows, (place + 1) * rows)
        lanes = slice(head * HEAD_DIM, (head + 1) * HEAD_DIM)
        grad = g_buf[:, lanes]
        q_tall[kv_head, spot, :] = q_buf[:, lanes]
        g_tall[kv_head, spot, :] = grad
        product = grad.astype(jnp.float32) * o_buf[:, lanes].astype(jnp.float32)
        dot_wide[kv_head : kv_head + 1, spot] = jnp.sum(product.T, axis=0, keepdims=True)
        lse_wide[kv_head : kv_head + 1, spot] = lse_ref[head : head + 1, :]
    order_all[me] = order_ref[...]

    last = order_ref[...]
    first = last - pos_ref[...]
    lane = lax.broadcasted_iota(jnp.int32, (1, rows), 1)
    place_in_block = lax.broadcasted_iota(jnp.int32, (rows, rows), 0)

    def block(member):
        start = order_all[member] - lane
        visible = (place_in_block <= last - start) & (place_in_block >= first - start)
        visible = jnp.concatenate([visible.astype(jnp.float32)] * group_size, axis=1) > 0.5
        for kv_head in range(kv_local):
            lanes = slice(kv_head * HEAD_DIM, (kv_head + 1) * HEAD_DIM)
            keys, values = k_all[member, :, lanes], v_all[member, :, lanes]
            queries, grads = q_tall[kv_head], g_tall[kv_head]
            scores = dot(keys, queries, ((1,), (1,))) * scale
            prob_grad = dot(values, grads, ((1,), (1,)))
            probs = jnp.where(visible, jnp.exp(scores - lse_wide[kv_head : kv_head + 1, :]), 0.0)
            score_grad = (
                probs * (prob_grad - dot_wide[kv_head : kv_head + 1, :]) * scale
            ).astype(jnp.bfloat16)
            ds_all[kv_head, pl.ds(pl.multiple_of(member * rows, rows), rows), :] = score_grad
            v_part[member, :, lanes] = dot(
                probs.astype(jnp.bfloat16), grads, ((1,), (0,))
            ).astype(jnp.bfloat16)
            k_part[member, :, lanes] = dot(score_grad, queries, ((1,), (0,))).astype(jnp.bfloat16)

    for head_step in range(1, groups):
        for which in range(2):
            kv_copy(which, me, head_at(head_step), me, head_at(head_step)).wait_recv()
    block(me)
    k_in[me, :, columns(mine)] = k_part[me, half(mine), :]
    v_in[me, :, columns(mine)] = v_part[me, half(mine), :]
    for head_step in range(1, groups):
        for which in range(2):
            grad_copy(which, me, head_at(head_step), me, mine).start()

    def visit(step):
        member = member_at(step)
        order_copy(member, member).wait_recv()
        for head_step in range(groups):
            for which in range(2):
                kv_copy(which, member, head_at(head_step), member, head_at(head_step)).wait_recv()
        block(member)
        for head_step in range(groups):
            for which in range(2):
                grad_copy(which, member, head_at(head_step), me, mine).start()

    loop(1, members, visit)

    keys_tall = k_all[...].reshape(members * rows, kv_columns)
    for kv_head in range(kv_local):
        keys = keys_tall[:, kv_head * HEAD_DIM : (kv_head + 1) * HEAD_DIM]
        update = dot(ds_all[kv_head], keys, ((0,), (0,))).astype(jnp.bfloat16)
        for place in range(group_size):
            head = kv_head * group_size + place
            dq_buf[:, head * HEAD_DIM : (head + 1) * HEAD_DIM] = update[
                place * rows : (place + 1) * rows, :
            ]
    dq_out = pltpu.make_async_copy(dq_buf, dq_hbm, local_sem.at[5])
    dq_out.start()

    def sent(step):
        member = member_at(step)
        order_copy(member, me).wait_send()
        for head_step in range(groups):
            for which in range(2):
                kv_copy(which, member, head_at(head_step), me, mine).wait_send()
                grad_copy(which, member, head_at(head_step), me, mine).wait_send()
                grad_copy(which, member, head_at(head_step), member, head_at(head_step)).wait_recv()

    for head_step in range(1, groups):
        for which in range(2):
            kv_copy(which, me, head_at(head_step), me, mine).wait_send()
            grad_copy(which, me, head_at(head_step), me, mine).wait_send()
            grad_copy(which, me, head_at(head_step), me, head_at(head_step)).wait_recv()
    loop(1, members, sent)

    outs = []
    for which, (inbox, buf, out) in enumerate(((k_in, dk_buf, dk_hbm), (v_in, dv_buf, dv_hbm))):
        buf[...] = jnp.sum(inbox[...].astype(jnp.float32), axis=0).astype(jnp.bfloat16)
        copy = pltpu.make_async_copy(buf, out, local_sem.at[6 + which])
        copy.start()
        outs.append(copy)
    dq_out.wait()
    for copy in outs:
        copy.wait()


def shards(
    queries, key_states, value_states, attn_out, grad_out, log_sum_exp, token_order, position
):
    members = lax.axis_size("ctx") // QUARTERS
    groups = lax.axis_size("head")
    rows, head_columns = queries.shape
    own, kv_total = key_states.shape
    kv_columns = kv_total // groups
    kv_local = kv_columns // HEAD_DIM
    wide = rows * (head_columns // kv_columns)
    anywhere = pl.BlockSpec(memory_space=pl.ANY)
    vmem = pl.BlockSpec(memory_space=pltpu.VMEM)
    bf16, f32 = jnp.bfloat16, jnp.float32
    dma = pltpu.SemaphoreType.DMA
    return pl.pallas_call(
        functools.partial(kernel, members, groups),
        out_shape=(
            jax.ShapeDtypeStruct(queries.shape, bf16),
            jax.ShapeDtypeStruct(key_states.shape, bf16),
            jax.ShapeDtypeStruct(value_states.shape, bf16),
        ),
        in_specs=[anywhere] * 5 + [vmem] * 3,
        out_specs=(anywhere,) * 3,
        scratch_shapes=[
            pltpu.VMEM((rows, head_columns), bf16),
            pltpu.VMEM((rows, head_columns), bf16),
            pltpu.VMEM((rows, head_columns), bf16),
            pltpu.VMEM((kv_local, wide, HEAD_DIM), bf16),
            pltpu.VMEM((kv_local, wide, HEAD_DIM), bf16),
            pltpu.VMEM((members, rows, kv_columns), bf16),
            pltpu.VMEM((members, rows, kv_columns), bf16),
            pltpu.VMEM((members, 1, rows), jnp.int32),
            pltpu.VMEM((kv_local, wide), f32),
            pltpu.VMEM((kv_local, wide), f32),
            pltpu.VMEM((kv_local, members * rows, wide), bf16),
            pltpu.VMEM((members, rows, kv_columns), bf16),
            pltpu.VMEM((members, rows, kv_columns), bf16),
            pltpu.VMEM((members, own, kv_total), bf16),
            pltpu.VMEM((members, own, kv_total), bf16),
            pltpu.VMEM((rows, head_columns), bf16),
            pltpu.VMEM((own, kv_total), bf16),
            pltpu.VMEM((own, kv_total), bf16),
            dma((8,)),
            dma((2, members, groups)),
            dma((2, members, groups)),
            dma((members,)),
            dma((members,)),
            dma((2, members, groups)),
            dma((2, members, groups)),
        ],
        compiler_params=pltpu.CompilerParams(
            collective_id=0, has_side_effects=True, vmem_limit_bytes=48 * 1024 * 1024
        ),
    )(
        queries, key_states, value_states, attn_out, grad_out, log_sum_exp,
        token_order.reshape(1, rows), position.reshape(1, rows),
    )


def solution(mesh):
    in_specs = (
        P("ctx", "head"),
        P(("ctx", "head"), None),
        P(("ctx", "head"), None),
        P("ctx", "head"),
        P("ctx", "head"),
        P("head", "ctx"),
        P("ctx"),
        P("ctx"),
    )
    out_specs = (P("ctx", "head"), P(("ctx", "head"), None), P(("ctx", "head"), None))
    return jax.shard_map(shards, mesh=mesh, in_specs=in_specs, out_specs=out_specs, check_vma=False)
```

```python
import functools

import jax
import jax.numpy as jnp
from jax import lax
from jax.experimental import pallas as pl
from jax.experimental.pallas import tpu as pltpu
from jax.sharding import PartitionSpec as P

HEAD_DIM = 128
QUARTERS = 4
MESH = pl.DeviceIdType.MESH


def dot(a, b, dims):
    return lax.dot_general(a, b, (dims, ((), ())), preferred_element_type=jnp.float32)


def kernel(
    members, groups,
    q_hbm, k_hbm, v_hbm, o_hbm, g_hbm, lse_ref, order_ref, pos_ref,
    dq_ref, dk_ref, dv_ref,
    q_buf, o_buf, g_buf, q_tall, g_tall, k_all, v_all, order_all,
    lse_wide, dot_wide, ds_all, part, inbox,
    local_sem, send_kv, recv_kv, send_order, recv_order, send_grad, recv_grad,
):
    ctx, mine = lax.axis_index("ctx"), lax.axis_index("head")
    me, quarter = ctx // QUARTERS, lax.rem(ctx, QUARTERS)
    own = k_hbm.shape[0]
    rows = q_hbm.shape[0]
    kv_columns = k_hbm.shape[1] // groups
    kv_local = kv_columns // HEAD_DIM
    group_size = q_hbm.shape[1] // kv_columns
    wide = group_size * rows
    scale = HEAD_DIM ** (-0.5)

    def loop(low, high, body):
        if members <= 4:
            for step in range(low, high):
                body(step)
        else:
            def call(step, carry):
                body(step)
                return carry
            lax.fori_loop(low, high, call, 0)

    def device(member, head):
        return (member * QUARTERS + quarter, head)

    def member_at(step):
        return lax.rem(me + step, members)

    def head_at(step):
        return lax.rem(mine + step, groups)

    def columns(head):
        return pl.ds(pl.multiple_of(head * kv_columns, kv_columns), kv_columns)

    def half(head):
        return pl.ds(pl.multiple_of(head * own, own), own)

    def kv_copy(which, member, head, sender, sender_head):
        source = (k_hbm, v_hbm)[which]
        target = (k_all, v_all)[which]
        return pltpu.make_async_remote_copy(
            src_ref=source.at[:, columns(head)],
            dst_ref=target.at[sender, half(sender_head)],
            send_sem=send_kv.at[which, member, head],
            recv_sem=recv_kv.at[which, sender, sender_head],
            device_id=device(member, head),
            device_id_type=MESH,
        )

    def order_copy(member, sender):
        return pltpu.make_async_remote_copy(
            src_ref=order_ref,
            dst_ref=order_all.at[sender],
            send_sem=send_order.at[member],
            recv_sem=recv_order.at[sender],
            device_id=device(member, mine),
            device_id_type=MESH,
        )

    def grad_copy(member, head, sender, sender_head):
        return pltpu.make_async_remote_copy(
            src_ref=part.at[member, head],
            dst_ref=inbox.at[sender, sender_head],
            send_sem=send_grad.at[member, head],
            recv_sem=recv_grad.at[sender, sender_head],
            device_id=device(member, head),
            device_id_type=MESH,
        )

    loads = [
        pltpu.make_async_copy(k_hbm.at[:, columns(mine)], k_all.at[me, half(mine)], local_sem.at[0]),
        pltpu.make_async_copy(v_hbm.at[:, columns(mine)], v_all.at[me, half(mine)], local_sem.at[1]),
        pltpu.make_async_copy(q_hbm, q_buf, local_sem.at[2]),
        pltpu.make_async_copy(o_hbm, o_buf, local_sem.at[3]),
        pltpu.make_async_copy(g_hbm, g_buf, local_sem.at[4]),
    ]
    for load in loads:
        load.start()

    barrier = pltpu.get_barrier_semaphore()

    def greet(step):
        for head_step in range(groups):
            def signal():
                pl.semaphore_signal(
                    barrier, inc=1, device_id=device(member_at(step), head_at(head_step)),
                    device_id_type=MESH,
                )
            signal()

    for head_step in range(1, groups):
        pl.semaphore_signal(
            barrier, inc=1, device_id=device(me, head_at(head_step)), device_id_type=MESH
        )
    loop(1, members, greet)
    pl.semaphore_wait(barrier, members * groups - 1)

    def push(step):
        member = member_at(step)
        order_copy(member, me).start()
        for head_step in range(groups):
            for which in range(2):
                kv_copy(which, member, head_at(head_step), me, mine).start()

    loop(1, members, push)
    for head_step in range(1, groups):
        for which in range(2):
            kv_copy(which, me, head_at(head_step), me, mine).start()

    for load in loads:
        load.wait()
    for head in range(group_size * kv_local):
        kv_head, place = head // group_size, head % group_size
        spot = slice(place * rows, (place + 1) * rows)
        lanes = slice(head * HEAD_DIM, (head + 1) * HEAD_DIM)
        grad = g_buf[:, lanes]
        q_tall[kv_head, spot, :] = q_buf[:, lanes]
        g_tall[kv_head, spot, :] = grad
        product = grad.astype(jnp.float32) * o_buf[:, lanes].astype(jnp.float32)
        dot_wide[kv_head : kv_head + 1, spot] = jnp.sum(product.T, axis=0, keepdims=True)
        lse_wide[kv_head : kv_head + 1, spot] = lse_ref[head : head + 1, :]
    order_all[me] = order_ref[...]

    last = order_ref[...]
    first = last - pos_ref[...]
    lane = lax.broadcasted_iota(jnp.int32, (1, rows), 1)
    place_in_block = lax.broadcasted_iota(jnp.int32, (rows, rows), 0)

    def block(member):
        start = order_all[member] - lane
        visible = (place_in_block <= last - start) & (place_in_block >= first - start)
        visible = jnp.concatenate([visible.astype(jnp.float32)] * group_size, axis=1) > 0.5
        for kv_head in range(kv_local):
            lanes = slice(kv_head * HEAD_DIM, (kv_head + 1) * HEAD_DIM)
            keys, values = k_all[member, :, lanes], v_all[member, :, lanes]
            queries, grads = q_tall[kv_head], g_tall[kv_head]
            scores = dot(keys, queries, ((1,), (1,))) * scale
            prob_grad = dot(values, grads, ((1,), (1,)))
            probs = jnp.where(visible, jnp.exp(scores - lse_wide[kv_head : kv_head + 1, :]), 0.0)
            score_grad = (
                probs * (prob_grad - dot_wide[kv_head : kv_head + 1, :]) * scale
            ).astype(jnp.bfloat16)
            ds_all[kv_head, pl.ds(pl.multiple_of(member * rows, rows), rows), :] = score_grad
            value_grad = dot(probs.astype(jnp.bfloat16), grads, ((1,), (0,)))
            key_grad = dot(score_grad, queries, ((1,), (0,)))
            for head in range(groups):
                spot = slice(head * own, (head + 1) * own)
                part[member, head, 0, :, lanes] = key_grad[spot].astype(jnp.bfloat16)
                part[member, head, 1, :, lanes] = value_grad[spot].astype(jnp.bfloat16)

    for head_step in range(1, groups):
        for which in range(2):
            kv_copy(which, me, head_at(head_step), me, head_at(head_step)).wait_recv()
    block(me)
    inbox[me, mine] = part[me, mine]
    for head_step in range(1, groups):
        grad_copy(me, head_at(head_step), me, mine).start()

    def visit(step):
        member = member_at(step)
        order_copy(member, member).wait_recv()
        for head_step in range(groups):
            for which in range(2):
                kv_copy(which, member, head_at(head_step), member, head_at(head_step)).wait_recv()
        block(member)
        for head_step in range(groups):
            grad_copy(member, head_at(head_step), me, mine).start()

    loop(1, members, visit)

    keys_tall = k_all[...].reshape(members * rows, kv_columns)
    for kv_head in range(kv_local):
        keys = keys_tall[:, kv_head * HEAD_DIM : (kv_head + 1) * HEAD_DIM]
        update = dot(ds_all[kv_head], keys, ((0,), (0,))).astype(jnp.bfloat16)
        for place in range(group_size):
            head = kv_head * group_size + place
            dq_ref[:, head * HEAD_DIM : (head + 1) * HEAD_DIM] = update[
                place * rows : (place + 1) * rows, :
            ]

    def sent(step):
        member = member_at(step)
        order_copy(member, me).wait_send()
        for head_step in range(groups):
            for which in range(2):
                kv_copy(which, member, head_at(head_step), me, mine).wait_send()
            grad_copy(member, head_at(head_step), me, mine).wait_send()
            grad_copy(member, head_at(head_step), member, head_at(head_step)).wait_recv()

    for head_step in range(1, groups):
        for which in range(2):
            kv_copy(which, me, head_at(head_step), me, mine).wait_send()
        grad_copy(me, head_at(head_step), me, mine).wait_send()
        grad_copy(me, head_at(head_step), me, head_at(head_step)).wait_recv()
    loop(1, members, sent)

    for head in range(groups):
        lanes = slice(head * kv_columns, (head + 1) * kv_columns)
        for which, out in enumerate((dk_ref, dv_ref)):
            total = jnp.sum(inbox[:, head, which].astype(jnp.float32), axis=0)
            out[:, lanes] = total.astype(jnp.bfloat16)


def shards(
    queries, key_states, value_states, attn_out, grad_out, log_sum_exp, token_order, position
):
    members = lax.axis_size("ctx") // QUARTERS
    groups = lax.axis_size("head")
    rows, head_columns = queries.shape
    own, kv_total = key_states.shape
    kv_columns = kv_total // groups
    kv_local = kv_columns // HEAD_DIM
    wide = rows * (head_columns // kv_columns)
    anywhere = pl.BlockSpec(memory_space=pl.ANY)
    vmem = pl.BlockSpec(memory_space=pltpu.VMEM)
    bf16, f32 = jnp.bfloat16, jnp.float32
    dma = pltpu.SemaphoreType.DMA
    return pl.pallas_call(
        functools.partial(kernel, members, groups),
        out_shape=(
            jax.ShapeDtypeStruct(queries.shape, bf16),
            jax.ShapeDtypeStruct(key_states.shape, bf16),
            jax.ShapeDtypeStruct(value_states.shape, bf16),
        ),
        in_specs=[anywhere] * 5 + [vmem] * 3,
        out_specs=(vmem,) * 3,
        scratch_shapes=[
            pltpu.VMEM((rows, head_columns), bf16),
            pltpu.VMEM((rows, head_columns), bf16),
            pltpu.VMEM((rows, head_columns), bf16),
            pltpu.VMEM((kv_local, wide, HEAD_DIM), bf16),
            pltpu.VMEM((kv_local, wide, HEAD_DIM), bf16),
            pltpu.VMEM((members, rows, kv_columns), bf16),
            pltpu.VMEM((members, rows, kv_columns), bf16),
            pltpu.VMEM((members, 1, rows), jnp.int32),
            pltpu.VMEM((kv_local, wide), f32),
            pltpu.VMEM((kv_local, wide), f32),
            pltpu.VMEM((kv_local, members * rows, wide), bf16),
            pltpu.VMEM((members, groups, 2, own, kv_columns), bf16),
            pltpu.VMEM((members, groups, 2, own, kv_columns), bf16),
            dma((5,)),
            dma((2, members, groups)),
            dma((2, members, groups)),
            dma((members,)),
            dma((members,)),
            dma((members, groups)),
            dma((members, groups)),
        ],
        compiler_params=pltpu.CompilerParams(
            collective_id=0, has_side_effects=True, vmem_limit_bytes=67043328
        ),
    )(
        queries, key_states, value_states, attn_out, grad_out, log_sum_exp,
        token_order.reshape(1, rows), position.reshape(1, rows),
    )


def solution(mesh):
    in_specs = (
        P("ctx", "head"),
        P(("ctx", "head"), None),
        P(("ctx", "head"), None),
        P("ctx", "head"),
        P("ctx", "head"),
        P("head", "ctx"),
        P("ctx"),
        P("ctx"),
    )
    out_specs = (P("ctx", "head"), P(("ctx", "head"), None), P(("ctx", "head"), None))
    return jax.shard_map(shards, mesh=mesh, in_specs=in_specs, out_specs=out_specs, check_vma=False)
```
